32 devices in a mesh: lat: 8 (over z, y), lon: 2 (over x), head: 2 (over core).
Axes of the slice: x: 2, y: 2, z: 4, core: 2. Of those that a mesh axis runs over, the one named last changes fastest.
Arguments:
- queries: bfloat16 [8, 2, 512, 1024], P('lat', 'lon', None, 'head'), may hold values from -250 to 250, as said below
- key_value: bfloat16 [8, 2, 512, 128], P('lat', 'lon'), may hold values from -5 to 5
- dout: bfloat16 [8, 2, 512, 1024], P('lat', 'lon', None, 'head'), may hold values from -6 to 6
Outputs:
- dquery: bfloat16 [8, 2, 512, 1024], P('lat', 'lon', None, 'head')
- dkey_value: float32 [8, 2, 512, 128], P('lat', 'lon', 'head')
The draws below stay inside these ranges and needn't reach their ends.
Inputs may be any that keep to these rules, and one draw needn't show every extreme that they name: `queries`: queries and keys have entries of order one, except that some query rows may be large multiples of nearby keys.
All inputs are finite; a program needn't handle non-finite values.
Results may differ from the reference program's by a relative error of at most 0.005.
Values may be sent and summed in bfloat16 or wider, within the bound.
A program may use at most 64 MiB of HBM per device.

```python
import jax
import jax.numpy as jnp
from jax import lax

HEADS = 16
HEAD_DIM = 64
TOK = 512
NLAT = 8
NLON = 2


def joint_draw(key):
    base = jax.random.fold_in(key, 11)
    first, second = jax.random.split(base, 2)
    pairs = jnp.clip(jax.random.normal(first, (NLAT, NLON, TOK, 2 * HEAD_DIM), jnp.float32), -5.0, 5.0)
    query_full = jnp.clip(jax.random.normal(second, (NLAT, NLON, TOK, HEADS, HEAD_DIM), jnp.float32), -5.0, 5.0)
    return (query_full.reshape(NLAT, NLON, TOK, HEADS * HEAD_DIM), pairs)


def draw_queries(key, part):
    return joint_draw(key)[0].astype(jnp.bfloat16)


def draw_key_value(key, part):
    return joint_draw(key)[1].astype(jnp.bfloat16)


def steps_of(own_key, dims, pieces, least, high):
    loudness = 1.0
    for dim, shards_of in pieces:
        draws = jax.random.uniform(jax.random.fold_in(jax.random.fold_in(own_key, 6), dim), (shards_of,), jnp.float32, least / len(pieces), high / len(pieces))
        loudness = loudness * jnp.repeat(jnp.exp(draws), dims[dim] // shards_of).reshape((-1,) + (1,) * (len(dims) - 1 - dim))
    return loudness


def gaussian(own_key, extent, width, limit, cuts=(), held_as=jnp.bfloat16):
    values = jax.random.normal(own_key, extent, jnp.float32) * width
    if len(cuts) > 0:
        values = steps_of(own_key, extent, cuts, -0.22, 0.18) * values
    return jnp.clip(values, min=-limit, max=limit).astype(held_as)


def setup_inputs(seed: int = 0) -> dict:
    streams_of = jax.random.split(jax.random.key(seed), 4)
    queries = draw_queries(jax.random.fold_in(streams_of[3], 71), 0)
    key_value = draw_key_value(jax.random.fold_in(streams_of[3], 71), 0)
    dout = gaussian(streams_of[2], (NLAT, NLON, TOK, HEADS * HEAD_DIM), 1.0, 6.0, ((0, 8), (1, 2), (3, 2)))
    return {"queries": queries, "key_value": key_value, "dout": dout}


def tile_grads(operands):
    query_tile, dout_tile, keys_tile = operands
    tokens = query_tile.shape[0]
    scale = 1.0 / (HEAD_DIM ** 0.5)
    q_heads = query_tile.reshape(tokens, HEADS, HEAD_DIM).astype(jnp.float32)
    d_heads = dout_tile.reshape(tokens, HEADS, HEAD_DIM).astype(jnp.float32)
    keys = keys_tile[:, :HEAD_DIM].astype(jnp.float32)
    values = keys_tile[:, HEAD_DIM:].astype(jnp.float32)
    scores = jnp.einsum("thd,kd->htk", q_heads, keys) * scale
    top = jnp.max(scores, axis=-1, keepdims=True)
    expo = jnp.exp(scores - top)
    probs = expo / jnp.sum(expo, axis=-1, keepdims=True)
    probs_low = lax.optimization_barrier(probs.astype(jnp.bfloat16)).astype(jnp.float32)
    dprobs = jnp.einsum("thd,kd->htk", d_heads, values)
    delta = jnp.sum(probs * dprobs, axis=-1, keepdims=True)
    dscore = lax.optimization_barrier((probs * (dprobs - delta) * scale).astype(jnp.bfloat16)).astype(jnp.float32)
    dquery = jnp.einsum("htk,kd->thd", dscore, keys).astype(jnp.bfloat16).reshape(tokens, HEADS * HEAD_DIM)
    dkeys = jnp.einsum("htk,thd->kd", dscore, q_heads)
    dvalues = jnp.einsum("htk,thd->kd", probs_low, d_heads)
    return dquery, jnp.concatenate([dkeys, dvalues], axis=1)


def reference(queries, key_value, dout):
    tiles = NLAT * NLON
    near = jnp.stack([key_value, jnp.roll(key_value, -2, 0), jnp.roll(key_value, 2, 0), jnp.roll(key_value, -2, 1), jnp.roll(key_value, 2, 1)], axis=2)
    near = near.reshape(tiles, 5 * TOK, 2 * HEAD_DIM)
    dquery, contrib = lax.map(tile_grads, (queries.reshape(tiles, TOK, HEADS * HEAD_DIM), dout.reshape(tiles, TOK, HEADS * HEAD_DIM), near))
    dquery = dquery.reshape(NLAT, NLON, TOK, HEADS * HEAD_DIM)
    contrib = contrib.reshape(NLAT, NLON, 5, TOK, 2 * HEAD_DIM)
    total = contrib[:, :, 0]
    total = total + jnp.roll(contrib[:, :, 1], 2, 0)
    total = total + jnp.roll(contrib[:, :, 2], -2, 0)
    total = total + jnp.roll(contrib[:, :, 3], 2, 1)
    total = total + jnp.roll(contrib[:, :, 4], -2, 1)
    return dquery, total
```

```python
import functools

import jax
import jax.numpy as jnp
from jax import lax
from jax.experimental import pallas as pl
from jax.experimental.pallas import tpu as pltpu
from jax.sharding import PartitionSpec as P

HEAD_DIM = 64
REACH = 2
MESH = pl.DeviceIdType.MESH
F32 = jnp.float32
BF16 = jnp.bfloat16


def tile_groups(n_lat, n_lon):
    counts = {}
    for dlat, dlon in ((0, 0), (REACH, 0), (-REACH, 0), (0, REACH), (0, -REACH)):
        at = (dlat % n_lat, dlon % n_lon)
        counts[at] = counts.get(at, 0) + 1
    return list(counts.items())


def kernel(
    groups, sizes, q_ref, kv_ref, d_ref, dq_ref, dkv_ref,
    kvb, feats, rhs, so, sa, sb, pown, pa, pb, acc, dqt, keyt, kept, xs, xr, gs, gr, xos, xor_,
    kv_send, kv_recv, fw_send, fw_recv, xs_send, xs_recv, g_send, g_recv, o_send, o_recv,
):
    n_lat, n_lon, n_head = sizes
    tok = kv_ref.shape[0]
    dim = HEAD_DIM
    n_heads = q_ref.shape[1] // dim
    part = tok // n_head
    n_near = len(groups) - 1
    scale = 1.0 / dim**0.5
    lat, lon, head = (lax.axis_index(a) for a in ("lat", "lon", "head"))
    mine = pl.ds(pl.multiple_of(head * part, part), part)

    def at(off, sign):
        return {
            "lat": lax.rem(lat + (sign * off[0]) % n_lat, n_lat),
            "lon": lax.rem(lon + (sign * off[1]) % n_lon, n_lon),
            "head": head,
        }

    def fellow(step):
        return {"lat": lat, "lon": lon, "head": lax.rem(head + step, n_head)}

    def send(src, dst, s_sem, r_sem, to):
        copy = pltpu.make_async_remote_copy(
            src_ref=src, dst_ref=dst, send_sem=s_sem, recv_sem=r_sem, device_id=to, device_id_type=MESH
        )
        copy.start()
        return copy

    barrier = pltpu.get_barrier_semaphore()
    for off, _ in groups[1:]:
        pl.semaphore_signal(barrier, inc=1, device_id=at(off, -1), device_id_type=MESH)
    for step in range(1, n_head):
        pl.semaphore_signal(barrier, inc=1, device_id=fellow(step), device_id_type=MESH)
    pl.semaphore_wait(barrier, n_near + n_head - 1)

    kv_copies = [
        send(kv_ref.at[mine], kvb.at[b, mine], kv_send.at[b], kv_recv.at[b], at(off, -1))
        for b, (off, _) in enumerate(groups[1:])
    ]

    lane = lax.broadcasted_iota(jnp.int32, (tok, 2 * dim), 1)
    low = lane < dim

    def prepare(i, carry):
        cols = pl.ds(pl.multiple_of(i * 2 * dim, 2 * dim), 2 * dim)
        q_two = q_ref[:, cols].astype(F32) * scale
        d_two = d_ref[:, cols].astype(F32)
        q_swap = jnp.concatenate([q_two[:, dim:], q_two[:, :dim]], axis=1)
        d_swap = jnp.concatenate([d_two[:, dim:], d_two[:, :dim]], axis=1)
        for k, (q_one, d_one) in enumerate(((q_two, d_swap), (q_swap, d_two))):
            q_low = jnp.where(low, q_one, 0.0).astype(BF16)
            d_high = jnp.where(low, 0.0, d_one).astype(BF16)
            feats[2 * i + k, :tok] = q_low
            feats[2 * i + k, tok:] = d_high
            rhs[2 * i + k, :, :tok] = q_low.T
            rhs[2 * i + k, :, tok:] = d_high.T
        for k in range(2):
            so[2 * i + k] = jnp.dot(kv_ref[...], rhs[2 * i + k], preferred_element_type=F32)
        return carry

    half = n_heads // 4
    keyt[0] = kv_ref[...].T[:dim]
    lax.fori_loop(0, half, prepare, 0)
    fw_copies = []
    for b in range(n_near):
        kv_copies[b].wait()
        for step in range(1, n_head):
            fw_copies.append(
                send(kvb.at[b, mine], kvb.at[b, mine], fw_send.at[b, step], fw_recv.at[b, step], fellow(step))
            )
    lax.fori_loop(half, n_heads // 2, prepare, 0)
    for copy in fw_copies:
        copy.wait()
    for b in range(n_near):
        keyt[1 + b] = kvb[b].T[:dim]

    def scores(h, s_ref):
        for b in range(n_near):
            s_ref[b] = jnp.dot(kvb[b], rhs[h], preferred_element_type=F32)

    rows, width = 64, 256

    def weights(h, s_ref, p_ref):
        for t in range(0, tok, width):
            s_cols, d_cols = pl.ds(t, width), pl.ds(tok + t, width)
            chunks = [(0, r) for r in range(0, tok, rows)] + [
                (1 + b, r) for b in range(n_near) for r in range(0, tok, rows)
            ]

            def load(b, r, cols):
                if b == 0:
                    return so[h, pl.ds(r, rows), cols]
                return s_ref[b - 1, pl.ds(r, rows), cols]

            def fold(x):
                return x.reshape(rows // 8, 8, width)

            top = None
            for b, r in chunks:
                m = jnp.max(fold(load(b, r, s_cols)), axis=0)
                top = m if top is None else jnp.maximum(top, m)
            top = jnp.max(top, axis=0, keepdims=True)
            sums, dots = 0.0, 0.0
            for b, (_, times) in enumerate(groups):
                l, e_d = 0.0, 0.0
                for r in range(0, tok, rows):
                    e = jnp.exp(load(b, r, s_cols) - top)
                    if b == 0:
                        so[h, pl.ds(r, rows), s_cols] = e
                    else:
                        s_ref[b - 1, pl.ds(r, rows), s_cols] = e
                    l = l + jnp.sum(fold(e), axis=0)
                    e_d = e_d + jnp.sum(fold(e * load(b, r, d_cols)), axis=0)
                sums = sums + times * l
                dots = dots + times * e_d
            total = jnp.sum(sums, axis=0, keepdims=True)
            inv = 1.0 / total
            delta = jnp.sum(dots, axis=0, keepdims=True) / total
            for b, r in chunks:
                p = load(b, r, s_cols) * inv
                ds = (p * (load(b, r, d_cols) - delta)).astype(BF16)
                if b == 0:
                    pown[h, pl.ds(r, rows), s_cols] = ds
                    pown[h, pl.ds(r, rows), d_cols] = p.astype(BF16)
                else:
                    p_ref[b - 1, pl.ds(r, rows), s_cols] = ds
                    p_ref[b - 1, pl.ds(r, rows), d_cols] = p.astype(BF16)

    def grads(h, p_ref):
        dq = jnp.dot(keyt[0], pown[h, :, :tok], preferred_element_type=F32) * (groups[0][1] * scale)
        for b in range(n_near):
            dq += jnp.dot(keyt[1 + b], p_ref[b, :, :tok], preferred_element_type=F32) * (groups[1 + b][1] * scale)
            acc[b] += jnp.dot(p_ref[b], feats[h], preferred_element_type=F32)
        dqt[h] = dq.astype(BF16)

    acc[...] = jnp.zeros_like(acc)

    def pair(i, carry):
        scores(2 * i, sa)
        scores(2 * i + 1, sb)
        weights(2 * i, sa, pa)
        weights(2 * i + 1, sb, pb)
        grads(2 * i, pa)
        grads(2 * i + 1, pb)
        return carry

    lax.fori_loop(0, n_heads // 2, pair, 0)

    def rows_of(step):
        return pl.ds(pl.multiple_of(lax.rem(head + step, n_head) * part, part), part)

    x_copies = []
    for b in range(n_near):
        for step in range(1, n_head):
            xs[b, step] = (acc[b, rows_of(step)] * groups[1 + b][1]).astype(BF16)
            x_copies.append(send(xs.at[b, step], xr.at[b, step], xs_send.at[b, step], xs_recv.at[b, step], fellow(step)))

    def own(h, total):
        return total + jnp.dot(pown[h], feats[h], preferred_element_type=F32)

    def own_into(first, last):
        kept[...] = lax.fori_loop(first, last, own, kept[...])

    kept[...] = jnp.zeros_like(kept)
    own_into(0, n_heads // 4)
    g_copies = []
    for copy in x_copies:
        copy.wait()
    for b, (off, times) in enumerate(groups[1:]):
        total = acc[b, mine] * times
        for step in range(1, n_head):
            total += xr[b, step].astype(F32)
        gs[b] = total.astype(BF16)
        g_copies.append(send(gs.at[b], gr.at[b], g_send.at[b], g_recv.at[b], at(off, 1)))
    own_into(n_heads // 4, n_heads)
    o_copies = []
    for step in range(1, n_head):
        xos[step] = kept[rows_of(step)]
        o_copies.append(send(xos.at[step], xor_.at[step], o_send.at[step], o_recv.at[step], fellow(step)))
    for j in range(n_heads // 2):
        two = jnp.concatenate([dqt[2 * j], dqt[2 * j + 1]], axis=0)
        dq_ref[:, 2 * dim * j : 2 * dim * (j + 1)] = two.T
    for copy in o_copies:
        copy.wait()
    total = kept[mine]
    for step in range(1, n_head):
        total += xor_[step]
    total = total * groups[0][1]
    for b, copy in enumerate(g_copies):
        copy.wait()
        total += gr[b].astype(F32)
    dkv_ref[...] = total


def local(sizes, queries, key_value, dout):
    n_head = sizes[2]
    tok, width = key_value.shape[2:]
    n_heads = queries.shape[3] // HEAD_DIM
    groups = tile_groups(sizes[0], sizes[1])
    near = max(len(groups) - 1, 1)
    part = tok // n_head
    vmem = pl.BlockSpec(memory_space=pltpu.VMEM)
    dma = pltpu.SemaphoreType.DMA
    keys = len(groups) * tok
    dq, dkv = pl.pallas_call(
        functools.partial(kernel, groups, sizes),
        out_shape=(
            jax.ShapeDtypeStruct((tok, n_heads * HEAD_DIM), BF16),
            jax.ShapeDtypeStruct((part, width), F32),
        ),
        in_specs=[vmem] * 3,
        out_specs=(vmem, vmem),
        scratch_shapes=[
            pltpu.VMEM((near, tok, width), BF16),
            pltpu.VMEM((n_heads, 2 * tok, width), BF16),
            pltpu.VMEM((n_heads, width, 2 * tok), BF16),
            pltpu.VMEM((n_heads, tok, 2 * tok), F32),
            pltpu.VMEM((near, tok, 2 * tok), F32),
            pltpu.VMEM((near, tok, 2 * tok), F32),
            pltpu.VMEM((n_heads, tok, 2 * tok), BF16),
            pltpu.VMEM((near, tok, 2 * tok), BF16),
            pltpu.VMEM((near, tok, 2 * tok), BF16),
            pltpu.VMEM((near, tok, width), F32),
            pltpu.VMEM((n_heads, HEAD_DIM, tok), BF16),
            pltpu.VMEM((near + 1, HEAD_DIM, tok), BF16),
            pltpu.VMEM((tok, width), F32),
            pltpu.VMEM((near, n_head, part, width), BF16),
            pltpu.VMEM((near, n_head, part, width), BF16),
            pltpu.VMEM((near, part, width), BF16),
            pltpu.VMEM((near, part, width), BF16),
            pltpu.VMEM((n_head, part, width), F32),
            pltpu.VMEM((n_head, part, width), F32),
            dma((near,)), dma((near,)),
            dma((near, n_head)), dma((near, n_head)),
            dma((near, n_head)), dma((near, n_head)),
            dma((near,)), dma((near,)),
            dma((n_head,)), dma((n_head,)),
        ],
        compiler_params=pltpu.CompilerParams(
            collective_id=0, has_side_effects=True, vmem_limit_bytes=60 * 2**20
        ),
        cost_estimate=pl.CostEstimate(
            flops=10 * n_heads * tok * keys * HEAD_DIM,
            bytes_accessed=8 * tok * n_heads * HEAD_DIM,
            transcendentals=n_heads * tok * keys,
        ),
    )(queries[0, 0], key_value[0, 0], dout[0, 0])
    return dq[None, None], dkv[None, None]


def solution(mesh):
    sizes = tuple(mesh.shape[a] for a in ("lat", "lon", "head"))
    placed = P("lat", "lon", None, "head")
    return jax.shard_map(
        functools.partial(local, sizes),
        mesh=mesh,
        in_specs=(placed, P("lat", "lon", None, None), placed),
        out_specs=(placed, P("lat", "lon", "head", None)),
        check_vma=False,
    )
```

```python
import functools

import jax
import jax.numpy as jnp
from jax import lax
from jax.experimental import pallas as pl
from jax.experimental.pallas import tpu as pltpu
from jax.sharding import PartitionSpec as P

HEAD_DIM = 64
REACH = 2
DEEP = 2
MESH = pl.DeviceIdType.MESH
F32 = jnp.float32
BF16 = jnp.bfloat16


def tile_groups(n_lat, n_lon):
    counts = {}
    for dlat, dlon in ((0, 0), (REACH, 0), (-REACH, 0), (0, REACH), (0, -REACH)):
        at = (dlat % n_lat, dlon % n_lon)
        counts[at] = counts.get(at, 0) + 1
    return list(counts.items())


def interleave(*lists):
    ranked = []
    for k, tasks in enumerate(lists):
        ranked += [((j + 0.5) / len(tasks), k, j) for j in range(len(tasks))]
    for _, k, j in sorted(ranked):
        lists[k][j]()


def kernel(
    groups, sizes, q_ref, kv_ref, d_ref, dq_ref, dkv_ref,
    kvb, rhs, feats, so, sa, sb, pown, pa, pb, fa, fb, mo, ma, mb, acc, dqn, invs, keyt, keyn, kept,
    xs, xr, gs, gr, xos, xor_,
    kv_send, kv_recv, fw_send, fw_recv, xs_send, xs_recv, g_send, g_recv, o_send, o_recv,
):
    n_lat, n_lon, n_head = sizes
    tok = kv_ref.shape[0]
    dim = HEAD_DIM
    n_heads = q_ref.shape[1] // dim
    part = tok // n_head
    n_near = len(groups) - 1
    scale = 1.0 / dim**0.5
    lat, lon, head = (lax.axis_index(a) for a in ("lat", "lon", "head"))
    mine = pl.ds(pl.multiple_of(head * part, part), part)

    def at(off, sign):
        return {
            "lat": lax.rem(lat + (sign * off[0]) % n_lat, n_lat),
            "lon": lax.rem(lon + (sign * off[1]) % n_lon, n_lon),
            "head": head,
        }

    def fellow(step):
        return {"lat": lat, "lon": lon, "head": lax.rem(head + step, n_head)}

    def send(src, dst, s_sem, r_sem, to):
        copy = pltpu.make_async_remote_copy(
            src_ref=src, dst_ref=dst, send_sem=s_sem, recv_sem=r_sem, device_id=to, device_id_type=MESH
        )
        copy.start()
        return copy

    barrier = pltpu.get_barrier_semaphore()
    for off, _ in groups[1:]:
        pl.semaphore_signal(barrier, inc=1, device_id=at(off, -1), device_id_type=MESH)
    for step in range(1, n_head):
        pl.semaphore_signal(barrier, inc=1, device_id=fellow(step), device_id_type=MESH)
    pl.semaphore_wait(barrier, n_near + n_head - 1)

    kv_copies = [
        send(kv_ref.at[mine], kvb.at[b, mine], kv_send.at[b], kv_recv.at[b], at(off, -1))
        for b, (off, _) in enumerate(groups[1:])
    ]

    def fold(x):
        return x.reshape(x.shape[0] // 8, 8, x.shape[1])

    above = jnp.zeros((dim, tok), BF16)

    def prepare(i, carry):
        cols = pl.ds(pl.multiple_of(i * 2 * dim, 2 * dim), 2 * dim)
        q_two = (q_ref[:, cols].astype(F32) * scale).astype(BF16).T
        d_two = d_ref[:, cols].T
        for k in range(2):
            h = 2 * i + k
            rhs[h, :dim, :tok] = q_two[k * dim : (k + 1) * dim]
            rhs[h, dim:, :tok] = above
            rhs[h, :dim, tok:] = above
            rhs[h, dim:, tok:] = d_two[k * dim : (k + 1) * dim]
        for k in range(2):
            h = 2 * i + k
            top = None
            for r in range(0, tok, piece):
                s = jnp.dot(kv_ref[pl.ds(r, piece)], rhs[h, :, :tok], preferred_element_type=F32)
                so[h, pl.ds(r, piece), :tok] = s
                m = jnp.max(fold(s), axis=0)
                top = m if top is None else jnp.maximum(top, m)
                so[h, pl.ds(r, piece), tok:] = jnp.dot(
                    kv_ref[pl.ds(r, piece)], rhs[h, :, tok:], preferred_element_type=F32
                )
            mo[h] = top
        return carry

    piece = tok // 2
    half = n_heads // 4
    keyt[...] = kv_ref[...].T[:dim]
    lax.fori_loop(0, half, prepare, 0)
    fw_copies = []
    for b in range(n_near):
        kv_copies[b].wait()
        for step in range(1, n_head):
            fw_copies.append(
                send(kvb.at[b, mine], kvb.at[b, mine], fw_send.at[b, step], fw_recv.at[b, step], fellow(step))
            )
    lax.fori_loop(half, n_heads // 2, prepare, 0)
    for copy in fw_copies:
        copy.wait()
    for b in range(n_near):
        keyn[:, pl.ds(b * tok, tok)] = (kvb[b].T[:dim].astype(F32) * groups[1 + b][1]).astype(BF16)

    def score_tasks(h, s_ref, m_ref):
        tasks = []
        for b in range(n_near):
            for r in range(0, tok, piece):

                def score(b=b, r=r):
                    s = jnp.dot(kvb[b, pl.ds(r, piece)], rhs[h, :, :tok], preferred_element_type=F32)
                    s_ref[pl.ds(b * tok + r, piece), :tok] = s
                    m = jnp.max(fold(s), axis=0)
                    m_ref[...] = m if b + r == 0 else jnp.maximum(m_ref[...], m)

                def gain(b=b, r=r):
                    s_ref[pl.ds(b * tok + r, piece), tok:] = jnp.dot(
                        kvb[b, pl.ds(r, piece)], rhs[h, :, tok:], preferred_element_type=F32
                    )

                tasks += [score, gain]
        return tasks

    rows, width = 64, tok // 2

    def weight_tasks(h, s_ref, m_ref, p_ref, f_ref):
        tasks = []
        tops = {}
        for t in range(0, tok, width):
            s_cols, d_cols = pl.ds(t, width), pl.ds(tok + t, width)
            state = {}

            def begin(t=t, state=state, s_cols=s_cols):
                state["top"] = jnp.max(jnp.maximum(mo[h, :, s_cols], m_ref[:, s_cols]), axis=0, keepdims=True)
                state["sums"], state["dots"] = 0.0, 0.0

            def first(b, r, state=state, s_cols=s_cols, d_cols=d_cols):
                if b == 0:
                    s, dp = so[h, pl.ds(r, rows), s_cols], so[h, pl.ds(r, rows), d_cols]
                else:
                    at_row = pl.ds((b - 1) * tok + r, rows)
                    s, dp = s_ref[at_row, s_cols], s_ref[at_row, d_cols]
                e = jnp.exp(s - state["top"])
                low = e.astype(BF16)
                if b == 0:
                    pown[h, pl.ds(r, rows), d_cols] = low
                else:
                    p_ref[at_row, d_cols] = low
                times = groups[b][1]
                if r == 0:
                    state["l"], state["e"] = 0.0, 0.0
                state["l"] += jnp.sum(fold(e), axis=0)
                state["e"] += jnp.sum(fold(e * dp), axis=0)
                if r + rows == tok:
                    state["sums"] += times * state["l"]
                    state["dots"] += times * state["e"]

            def middle(t=t, state=state, s_cols=s_cols, d_cols=d_cols):
                total = jnp.sum(state["sums"], axis=0, keepdims=True)
                state["delta"] = jnp.sum(state["dots"], axis=0, keepdims=True) / total
                inv = 1.0 / total
                invs[h, :, s_cols] = inv
                for base, cols in ((t, s_cols), (tok + t, d_cols)):
                    scaled = (rhs[h, :, cols].astype(F32) * inv).astype(BF16).T
                    f_ref[pl.ds(base, width)] = scaled
                    feats[h, pl.ds(base, width)] = scaled

            def second(b, r, state=state, s_cols=s_cols, d_cols=d_cols):
                if b == 0:
                    low, dp = pown[h, pl.ds(r, rows), d_cols], so[h, pl.ds(r, rows), d_cols]
                    pown[h, pl.ds(r, rows), s_cols] = low * (dp - state["delta"]).astype(BF16)
                else:
                    at_row = pl.ds((b - 1) * tok + r, rows)
                    low, dp = p_ref[at_row, d_cols], s_ref[at_row, d_cols]
                    p_ref[at_row, s_cols] = low * (dp - state["delta"]).astype(BF16)

            chunks = [(b, r) for b in range(n_near + 1) for r in range(0, tok, rows)]
            tasks.append(begin)
            tasks += [functools.partial(first, b, r) for b, r in chunks]
            tasks.append(middle)
            tasks += [functools.partial(second, b, r) for b, r in chunks]
        return tasks

    def grad_tasks(h, p_ref, f_ref):
        tasks = []
        for b in range(n_near):
            for r in range(0, tok, piece):

                def grad(b=b, r=r):
                    acc[b, pl.ds(r, piece)] += jnp.dot(
                        p_ref[pl.ds(b * tok + r, piece)], f_ref[...], preferred_element_type=F32
                    )

                tasks.append(grad)

        def to_queries():
            dqn[h] = jnp.dot(keyn[...], p_ref[:, :tok], preferred_element_type=F32)

        if n_near:
            tasks.append(to_queries)
        return tasks

    acc[...] = jnp.zeros_like(acc)
    if not n_near:
        dqn[...] = jnp.zeros_like(dqn)
        ma[...] = jnp.full_like(ma, -jnp.inf)
        mb[...] = jnp.full_like(mb, -jnp.inf)
    even, odd = (sa, ma, pa, fa), (sb, mb, pb, fb)

    if n_near > DEEP:

        def one(h, carry):
            for tasks in (score_tasks(h, sa, ma), weight_tasks(h, *even), grad_tasks(h, pa, fa)):
                interleave(tasks)
            return carry

        lax.fori_loop(0, n_heads, one, 0)
    else:
        interleave(score_tasks(0, sa, ma))
        interleave(weight_tasks(0, *even), score_tasks(1, sb, mb))

        def pair(i, carry):
            h = 2 * i + 1
            interleave(weight_tasks(h, *odd), grad_tasks(h - 1, pa, fa) + score_tasks(h + 1, sa, ma))
            interleave(weight_tasks(h + 1, *even), grad_tasks(h, pb, fb) + score_tasks(h + 2, sb, mb))
            return carry

        lax.fori_loop(0, n_heads // 2 - 1, pair, 0)
        last = n_heads - 1
        interleave(weight_tasks(last, *odd), grad_tasks(last - 1, pa, fa))
        interleave(grad_tasks(last, pb, fb))

    def rows_of(step):
        return pl.ds(pl.multiple_of(lax.rem(head + step, n_head) * part, part), part)

    x_copies = []
    for b in range(n_near):
        for step in range(1, n_head):
            xs[b, step] = (acc[b, rows_of(step)] * groups[1 + b][1]).astype(BF16)
            x_copies.append(send(xs.at[b, step], xr.at[b, step], xs_send.at[b, step], xs_recv.at[b, step], fellow(step)))

    def own_pair(i, carry):
        for r in range(0, tok, piece):
            kept[pl.ds(r, piece)] += jnp.dot(
                pown[2 * i, pl.ds(r, piece)], feats[2 * i], preferred_element_type=F32
            ) + jnp.dot(pown[2 * i + 1, pl.ds(r, piece)], feats[2 * i + 1], preferred_element_type=F32)
        both = []
        for h in (2 * i, 2 * i + 1):
            dq = jnp.dot(keyt[...], pown[h, :, :tok], preferred_element_type=F32) * groups[0][1] + dqn[h]
            both.append((dq * (invs[h] * scale)).astype(BF16))
        cols = pl.ds(pl.multiple_of(i * 2 * dim, 2 * dim), 2 * dim)
        dq_ref[:, cols] = jnp.concatenate(both, axis=0).T
        return carry

    kept[...] = jnp.zeros_like(kept)
    lax.fori_loop(0, n_heads // 8, own_pair, 0)
    g_copies = []
    for copy in x_copies:
        copy.wait()
    for b, (off, times) in enumerate(groups[1:]):
        total = acc[b, mine] * times
        for step in range(1, n_head):
            total += xr[b, step].astype(F32)
        gs[b] = total.astype(BF16)
        g_copies.append(send(gs.at[b], gr.at[b], g_send.at[b], g_recv.at[b], at(off, 1)))
    lax.fori_loop(n_heads // 8, n_heads // 2, own_pair, 0)
    o_copies = []
    for step in range(1, n_head):
        xos[step] = kept[rows_of(step)]
        o_copies.append(send(xos.at[step], xor_.at[step], o_send.at[step], o_recv.at[step], fellow(step)))
    for copy in o_copies:
        copy.wait()
    total = kept[mine]
    for step in range(1, n_head):
        total += xor_[step]
    total = total * groups[0][1]
    for b, copy in enumerate(g_copies):
        copy.wait()
        total += gr[b].astype(F32)
    dkv_ref[...] = total


def local(sizes, queries, key_value, dout):
    n_head = sizes[2]
    tok, width = key_value.shape[2:]
    n_heads = queries.shape[3] // HEAD_DIM
    groups = tile_groups(sizes[0], sizes[1])
    near = max(len(groups) - 1, 1)
    second = near * tok if near <= DEEP else 16
    part = tok // n_head
    vmem = pl.BlockSpec(memory_space=pltpu.VMEM)
    dma = pltpu.SemaphoreType.DMA
    keys = len(groups) * tok
    dq, dkv = pl.pallas_call(
        functools.partial(kernel, groups, sizes),
        out_shape=(
            jax.ShapeDtypeStruct((tok, n_heads * HEAD_DIM), BF16),
            jax.ShapeDtypeStruct((part, width), F32),
        ),
        in_specs=[vmem] * 3,
        out_specs=(vmem, vmem),
        scratch_shapes=[
            pltpu.VMEM((near, tok, width), BF16),
            pltpu.VMEM((n_heads, width, 2 * tok), BF16),
            pltpu.VMEM((n_heads, 2 * tok, width), BF16),
            pltpu.VMEM((n_heads, tok, 2 * tok), F32),
            pltpu.VMEM((near * tok, 2 * tok), F32),
            pltpu.VMEM((second, 2 * tok), F32),
            pltpu.VMEM((n_heads, tok, 2 * tok), BF16),
            pltpu.VMEM((near * tok, 2 * tok), BF16),
            pltpu.VMEM((second, 2 * tok), BF16),
            pltpu.VMEM((2 * tok, width), BF16),
            pltpu.VMEM((2 * tok, width), BF16),
            pltpu.VMEM((n_heads, 8, tok), F32),
            pltpu.VMEM((8, tok), F32),
            pltpu.VMEM((8, tok), F32),
            pltpu.VMEM((near, tok, width), F32),
            pltpu.VMEM((n_heads, HEAD_DIM, tok), F32),
            pltpu.VMEM((n_heads, 1, tok), F32),
            pltpu.VMEM((HEAD_DIM, tok), BF16),
            pltpu.VMEM((HEAD_DIM, near * tok), BF16),
            pltpu.VMEM((tok, width), F32),
            pltpu.VMEM((near, n_head, part, width), BF16),
            pltpu.VMEM((near, n_head, part, width), BF16),
            pltpu.VMEM((near, part, width), BF16),
            pltpu.VMEM((near, part, width), BF16),
            pltpu.VMEM((n_head, part, width), F32),
            pltpu.VMEM((n_head, part, width), F32),
            dma((near,)), dma((near,)),
            dma((near, n_head)), dma((near, n_head)),
            dma((near, n_head)), dma((near, n_head)),
            dma((near,)), dma((near,)),
            dma((n_head,)), dma((n_head,)),
        ],
        compiler_params=pltpu.CompilerParams(
            collective_id=0, has_side_effects=True, vmem_limit_bytes=62 * 2**20
        ),
        cost_estimate=pl.CostEstimate(
            flops=10 * n_heads * tok * keys * HEAD_DIM,
            bytes_accessed=8 * tok * n_heads * HEAD_DIM,
            transcendentals=n_heads * tok * keys,
        ),
    )(queries[0, 0], key_value[0, 0], dout[0, 0])
    return dq[None, None], dkv[None, None]


def solution(mesh):
    sizes = tuple(mesh.shape[a] for a in ("lat", "lon", "head"))
    placed = P("lat", "lon", None, "head")
    return jax.shard_map(
        functools.partial(local, sizes),
        mesh=mesh,
        in_specs=(placed, P("lat", "lon", None, None), placed),
        out_specs=(placed, P("lat", "lon", "head", None)),
        check_vma=False,
    )
```

```python
import functools

import jax
import jax.numpy as jnp
from jax import lax
from jax.experimental import pallas as pl
from jax.experimental.pallas import tpu as pltpu
from jax.sharding import PartitionSpec as P

HEAD_DIM = 64
REACH = 2
DEEP = 2
MESH = pl.DeviceIdType.MESH
F32 = jnp.float32
BF16 = jnp.bfloat16


def tile_groups(n_lat, n_lon):
    counts = {}
    for dlat, dlon in ((0, 0), (REACH, 0), (-REACH, 0), (0, REACH), (0, -REACH)):
        at = (dlat % n_lat, dlon % n_lon)
        counts[at] = counts.get(at, 0) + 1
    return list(counts.items())


def interleave(*lists):
    ranked = []
    for k, tasks in enumerate(lists):
        ranked += [((j + 0.5) / len(tasks), k, j) for j in range(len(tasks))]
    for _, k, j in sorted(ranked):
        lists[k][j]()


def kernel(
    groups, sizes, q_ref, kv_ref, d_ref, dq_ref, dkv_ref,
    kvb, rhs, feats, so, sa, sb, pown, pa, pb, fa, fb, mo, ma, mb, acc, dqn, invs, delta, keyt, keyn, kept,
    xs, xr, gs, gr, xos, xor_,
    kv_send, kv_recv, fw_send, fw_recv, xs_send, xs_recv, g_send, g_recv, o_send, o_recv,
):
    n_lat, n_lon, n_head = sizes
    tok = kv_ref.shape[0]
    dim = HEAD_DIM
    n_heads = q_ref.shape[1] // dim
    part = tok // n_head
    n_near = len(groups) - 1
    scale = 1.0 / dim**0.5
    lat, lon, head = (lax.axis_index(a) for a in ("lat", "lon", "head"))
    mine = pl.ds(pl.multiple_of(head * part, part), part)

    def at(off, sign):
        return {
            "lat": lax.rem(lat + (sign * off[0]) % n_lat, n_lat),
            "lon": lax.rem(lon + (sign * off[1]) % n_lon, n_lon),
            "head": head,
        }

    def fellow(step):
        return {"lat": lat, "lon": lon, "head": lax.rem(head + step, n_head)}

    def send(src, dst, s_sem, r_sem, to):
        copy = pltpu.make_async_remote_copy(
            src_ref=src, dst_ref=dst, send_sem=s_sem, recv_sem=r_sem, device_id=to, device_id_type=MESH
        )
        copy.start()
        return copy

    barrier = pltpu.get_barrier_semaphore()
    for off, _ in groups[1:]:
        pl.semaphore_signal(barrier, inc=1, device_id=at(off, -1), device_id_type=MESH)
    for step in range(1, n_head):
        pl.semaphore_signal(barrier, inc=1, device_id=fellow(step), device_id_type=MESH)
    pl.semaphore_wait(barrier, n_near + n_head - 1)

    kv_copies = [
        send(kv_ref.at[mine], kvb.at[b, mine], kv_send.at[b], kv_recv.at[b], at(off, -1))
        for b, (off, _) in enumerate(groups[1:])
    ]

    def fold(x):
        return x.reshape(x.shape[0] // 8, 8, x.shape[1])

    above = jnp.zeros((dim, tok), BF16)

    def prepare(i, carry):
        cols = pl.ds(pl.multiple_of(i * 2 * dim, 2 * dim), 2 * dim)
        q_two = (q_ref[:, cols].astype(F32) * scale).astype(BF16).T
        d_two = d_ref[:, cols].T
        for k in range(2):
            h = 2 * i + k
            rhs[h, :dim, :tok] = q_two[k * dim : (k + 1) * dim]
            rhs[h, dim:, :tok] = above
            rhs[h, :dim, tok:] = above
            rhs[h, dim:, tok:] = d_two[k * dim : (k + 1) * dim]
        for k in range(2):
            h = 2 * i + k
            top = None
            for r in range(0, tok, piece):
                s = jnp.dot(kv_ref[pl.ds(r, piece)], rhs[h, :, :tok], preferred_element_type=F32)
                so[h, pl.ds(r, piece), :tok] = s
                m = jnp.max(fold(s), axis=0)
                top = m if top is None else jnp.maximum(top, m)
                so[h, pl.ds(r, piece), tok:] = jnp.dot(
                    kv_ref[pl.ds(r, piece)], rhs[h, :, tok:], preferred_element_type=F32
                )
            mo[h] = top
        return carry

    piece = tok
    half = n_heads // 4
    keyt[...] = kv_ref[...].T[:dim]
    lax.fori_loop(0, half, prepare, 0)
    fw_copies = []
    for b in range(n_near):
        kv_copies[b].wait()
        for step in range(1, n_head):
            fw_copies.append(
                send(kvb.at[b, mine], kvb.at[b, mine], fw_send.at[b, step], fw_recv.at[b, step], fellow(step))
            )
    lax.fori_loop(half, n_heads // 2, prepare, 0)
    for copy in fw_copies:
        copy.wait()
    for b in range(n_near):
        keyn[:, pl.ds(b * tok, tok)] = (kvb[b].T[:dim].astype(F32) * groups[1 + b][1]).astype(BF16)

    def score_tasks(h, s_ref, m_ref):
        tasks = []
        for b in range(n_near):
            for r in range(0, tok, piece):

                def score(b=b, r=r):
                    s = jnp.dot(kvb[b, pl.ds(r, piece)], rhs[h, :, :tok], preferred_element_type=F32)
                    s_ref[pl.ds(b * tok + r, piece), :tok] = s
                    m = jnp.max(fold(s), axis=0)
                    m_ref[...] = m if b + r == 0 else jnp.maximum(m_ref[...], m)

                def gain(b=b, r=r):
                    s_ref[pl.ds(b * tok + r, piece), tok:] = jnp.dot(
                        kvb[b, pl.ds(r, piece)], rhs[h, :, tok:], preferred_element_type=F32
                    )

                tasks += [score, gain]
        return tasks

    rows, width = 64, tok // 2

    def near_rows(b, r):
        return pl.ds((b - 1) * tok + r, rows)

    chunks = [(b, r) for b in range(n_near + 1) for r in range(0, tok, rows)]

    def first_tasks(h, s_ref, m_ref, p_ref, f_ref):
        tasks = []
        for t in range(0, tok, width):
            s_cols, d_cols = pl.ds(t, width), pl.ds(tok + t, width)
            state = {}

            def begin(state=state, s_cols=s_cols):
                state["top"] = jnp.max(jnp.maximum(mo[h, :, s_cols], m_ref[:, s_cols]), axis=0, keepdims=True)
                state["sums"], state["dots"] = 0.0, 0.0

            def first(b, r, state=state, s_cols=s_cols, d_cols=d_cols):
                if b == 0:
                    s, dp = so[h, pl.ds(r, rows), s_cols], so[h, pl.ds(r, rows), d_cols]
                else:
                    s, dp = s_ref[near_rows(b, r), s_cols], s_ref[near_rows(b, r), d_cols]
                e = jnp.exp(s - state["top"])
                if b == 0:
                    pown[h, pl.ds(r, rows), d_cols] = e.astype(BF16)
                else:
                    p_ref[near_rows(b, r), d_cols] = e.astype(BF16)
                if r == 0:
                    state["l"], state["e"] = 0.0, 0.0
                state["l"] += jnp.sum(fold(e), axis=0)
                state["e"] += jnp.sum(fold(e * dp), axis=0)
                if r + rows == tok:
                    state["sums"] += groups[b][1] * state["l"]
                    state["dots"] += groups[b][1] * state["e"]

            def finish(state=state, s_cols=s_cols):
                total = jnp.sum(state["sums"], axis=0, keepdims=True)
                delta[:, s_cols] = jnp.sum(state["dots"], axis=0, keepdims=True) / total
                invs[h, :, s_cols] = 1.0 / total

            tasks.append(begin)
            tasks += [functools.partial(first, b, r) for b, r in chunks]
            tasks.append(finish)
        return tasks

    def second_tasks(h, s_ref, m_ref, p_ref, f_ref):
        tasks = []
        for t in range(0, tok, width):
            s_cols, d_cols = pl.ds(t, width), pl.ds(tok + t, width)

            def features(t=t, s_cols=s_cols, d_cols=d_cols):
                inv = invs[h, :, s_cols]
                for base, cols in ((t, s_cols), (tok + t, d_cols)):
                    scaled = (rhs[h, :, cols].astype(F32) * inv).astype(BF16).T
                    f_ref[pl.ds(base, width)] = scaled
                    feats[h, pl.ds(base, width)] = scaled

            def second(b, r, s_cols=s_cols, d_cols=d_cols):
                if b == 0:
                    low, dp = pown[h, pl.ds(r, rows), d_cols], so[h, pl.ds(r, rows), d_cols]
                else:
                    low, dp = p_ref[near_rows(b, r), d_cols], s_ref[near_rows(b, r), d_cols]
                ds = (low.astype(F32) * (dp - delta[:, s_cols])).astype(BF16)
                if b == 0:
                    pown[h, pl.ds(r, rows), s_cols] = ds
                else:
                    p_ref[near_rows(b, r), s_cols] = ds

            tasks.append(features)
            tasks += [functools.partial(second, b, r) for b, r in chunks]
        return tasks

    def grad_tasks(h, p_ref, f_ref):
        tasks = []
        for b in range(n_near):
            for r in range(0, tok, piece):

                def grad(b=b, r=r):
                    acc[b, pl.ds(r, piece)] += jnp.dot(
                        p_ref[pl.ds(b * tok + r, piece)], f_ref[...], preferred_element_type=F32
                    )

                tasks.append(grad)

        def to_queries():
            dqn[h] = jnp.dot(keyn[...], p_ref[:, :tok], preferred_element_type=F32)

        if n_near:
            tasks.append(to_queries)
        return tasks

    acc[...] = jnp.zeros_like(acc)
    if not n_near:
        dqn[...] = jnp.zeros_like(dqn)
        ma[...] = jnp.full_like(ma, -jnp.inf)
        mb[...] = jnp.full_like(mb, -jnp.inf)
    even, odd = (sa, ma, pa, fa), (sb, mb, pb, fb)

    def block(*lists):
        @pl.when(lat >= 0)
        def _():
            interleave(*lists)

    if n_near > DEEP:

        def one(h, carry):
            block(score_tasks(h, sa, ma))
            block(first_tasks(h, *even))
            block(second_tasks(h, *even))
            block(grad_tasks(h, pa, fa))
            return carry

        lax.fori_loop(0, n_heads, one, 0)
    else:
        block(score_tasks(0, sa, ma))
        block(first_tasks(0, *even), score_tasks(1, sb, mb))
        block(second_tasks(0, *even))

        def pair(i, carry):
            h = 2 * i + 1
            block(first_tasks(h, *odd), score_tasks(h + 1, sa, ma))
            block(second_tasks(h, *odd), grad_tasks(h - 1, pa, fa))
            block(first_tasks(h + 1, *even), score_tasks(h + 2, sb, mb))
            block(second_tasks(h + 1, *even), grad_tasks(h, pb, fb))
            return carry

        lax.fori_loop(0, n_heads // 2 - 1, pair, 0)
        last = n_heads - 1
        block(first_tasks(last, *odd))
        block(second_tasks(last, *odd), grad_tasks(last - 1, pa, fa))
        block(grad_tasks(last, pb, fb))

    def rows_of(step):
        return pl.ds(pl.multiple_of(lax.rem(head + step, n_head) * part, part), part)

    x_copies = []
    for b in range(n_near):
        for step in range(1, n_head):
            xs[b, step] = (acc[b, rows_of(step)] * groups[1 + b][1]).astype(BF16)
            x_copies.append(send(xs.at[b, step], xr.at[b, step], xs_send.at[b, step], xs_recv.at[b, step], fellow(step)))

    def own_pair(i, carry):
        for r in range(0, tok, piece):
            kept[pl.ds(r, piece)] += jnp.dot(
                pown[2 * i, pl.ds(r, piece)], feats[2 * i], preferred_element_type=F32
            ) + jnp.dot(pown[2 * i + 1, pl.ds(r, piece)], feats[2 * i + 1], preferred_element_type=F32)
        both = []
        for h in (2 * i, 2 * i + 1):
            dq = jnp.dot(keyt[...], pown[h, :, :tok], preferred_element_type=F32) * groups[0][1] + dqn[h]
            both.append(dq * (invs[h] * scale))
        cols = pl.ds(pl.multiple_of(i * 2 * dim, 2 * dim), 2 * dim)
        dq_ref[:, cols] = jnp.concatenate(both, axis=0).T
        return carry

    kept[...] = jnp.zeros_like(kept)
    lax.fori_loop(0, n_heads // 8, own_pair, 0)
    g_copies = []
    for copy in x_copies:
        copy.wait()
    for b, (off, times) in enumerate(groups[1:]):
        total = acc[b, mine] * times
        for step in range(1, n_head):
            total += xr[b, step].astype(F32)
        gs[b] = total.astype(BF16)
        g_copies.append(send(gs.at[b], gr.at[b], g_send.at[b], g_recv.at[b], at(off, 1)))
    lax.fori_loop(n_heads // 8, n_heads // 2, own_pair, 0)
    o_copies = []
    for step in range(1, n_head):
        xos[step] = kept[rows_of(step)]
        o_copies.append(send(xos.at[step], xor_.at[step], o_send.at[step], o_recv.at[step], fellow(step)))
    for copy in o_copies:
        copy.wait()
    total = kept[mine]
    for step in range(1, n_head):
        total += xor_[step]
    dkv_ref[0] = total * groups[0][1]
    total = jnp.zeros_like(total)
    for b, copy in enumerate(g_copies):
        copy.wait()
        total += gr[b].astype(F32)
    dkv_ref[1] = total


def local(sizes, queries, key_value, dout):
    n_head = sizes[2]
    tok, width = key_value.shape[2:]
    n_heads = queries.shape[3] // HEAD_DIM
    groups = tile_groups(sizes[0], sizes[1])
    near = max(len(groups) - 1, 1)
    second = near * tok if near <= DEEP else 16
    part = tok // n_head
    vmem = pl.BlockSpec(memory_space=pltpu.VMEM)
    dma = pltpu.SemaphoreType.DMA
    keys = len(groups) * tok
    dq, dkv = pl.pallas_call(
        functools.partial(kernel, groups, sizes),
        out_shape=(
            jax.ShapeDtypeStruct((tok, n_heads * HEAD_DIM), F32),
            jax.ShapeDtypeStruct((2, part, width), F32),
        ),
        in_specs=[vmem] * 3,
        out_specs=(vmem, vmem),
        scratch_shapes=[
            pltpu.VMEM((near, tok, width), BF16),
            pltpu.VMEM((n_heads, width, 2 * tok), BF16),
            pltpu.VMEM((n_heads, 2 * tok, width), BF16),
            pltpu.VMEM((n_heads, tok, 2 * tok), F32),
            pltpu.VMEM((near * tok, 2 * tok), F32),
            pltpu.VMEM((second, 2 * tok), F32),
            pltpu.VMEM((n_heads, tok, 2 * tok), BF16),
            pltpu.VMEM((near * tok, 2 * tok), BF16),
            pltpu.VMEM((second, 2 * tok), BF16),
            pltpu.VMEM((2 * tok, width), BF16),
            pltpu.VMEM((2 * tok, width), BF16),
            pltpu.VMEM((n_heads, 8, tok), F32),
            pltpu.VMEM((8, tok), F32),
            pltpu.VMEM((8, tok), F32),
            pltpu.VMEM((near, tok, width), F32),
            pltpu.VMEM((n_heads, HEAD_DIM, tok), F32),
            pltpu.VMEM((n_heads, 1, tok), F32),
            pltpu.VMEM((1, tok), F32),
            pltpu.VMEM((HEAD_DIM, tok), BF16),
            pltpu.VMEM((HEAD_DIM, near * tok), BF16),
            pltpu.VMEM((tok, width), F32),
            pltpu.VMEM((near, n_head, part, width), BF16),
            pltpu.VMEM((near, n_head, part, width), BF16),
            pltpu.VMEM((near, part, width), BF16),
            pltpu.VMEM((near, part, width), BF16),
            pltpu.VMEM((n_head, part, width), F32),
            pltpu.VMEM((n_head, part, width), F32),
            dma((near,)), dma((near,)),
            dma((near, n_head)), dma((near, n_head)),
            dma((near, n_head)), dma((near, n_head)),
            dma((near,)), dma((near,)),
            dma((n_head,)), dma((n_head,)),
        ],
        compiler_params=pltpu.CompilerParams(
            collective_id=0, has_side_effects=True, vmem_limit_bytes=62 * 2**20
        ),
        cost_estimate=pl.CostEstimate(
            flops=10 * n_heads * tok * keys * HEAD_DIM,
            bytes_accessed=8 * tok * n_heads * HEAD_DIM,
            transcendentals=n_heads * tok * keys,
        ),
    )(queries[0, 0], key_value[0, 0], dout[0, 0])
    return dq.astype(BF16)[None, None], (dkv[0] + dkv[1])[None, None]


def solution(mesh):
    sizes = tuple(mesh.shape[a] for a in ("lat", "lon", "head"))
    placed = P("lat", "lon", None, "head")
    return jax.shard_map(
        functools.partial(local, sizes),
        mesh=mesh,
        in_specs=(placed, P("lat", "lon", None, None), placed),
        out_specs=(placed, P("lat", "lon", "head", None)),
        check_vma=False,
    )
```

```python
import functools

import jax
import jax.numpy as jnp
from jax import lax
from jax.experimental import pallas as pl
from jax.experimental.pallas import tpu as pltpu
from jax.sharding import PartitionSpec as P

HEAD_DIM = 64
REACH = 2
DEEP = 2
MESH = pl.DeviceIdType.MESH
F32 = jnp.float32
BF16 = jnp.bfloat16


def tile_groups(n_lat, n_lon):
    counts = {}
    for dlat, dlon in ((0, 0), (REACH, 0), (-REACH, 0), (0, REACH), (0, -REACH)):
        at = (dlat % n_lat, dlon % n_lon)
        counts[at] = counts.get(at, 0) + 1
    return list(counts.items())


def interleave(*lists):
    ranked = []
    for k, tasks in enumerate(lists):
        ranked += [((j + 0.5) / len(tasks), k, j) for j in range(len(tasks))]
    for _, k, j in sorted(ranked):
        lists[k][j]()


def kernel(
    groups, sizes, q_ref, kv_ref, d_ref, dq_ref, dkv_ref,
    kvb, rhs, feats, so, sa, sb, pown, pa, pb, fa, fb, mo, ma, mb, acc, dqn, invs, delta, keyt, keyn, kept,
    xs, xr, gs, gr, xos, xor_,
    kv_send, kv_recv, fw_send, fw_recv, xs_send, xs_recv, g_send, g_recv, o_send, o_recv,
):
    n_lat, n_lon, n_head = sizes
    tok = kv_ref.shape[0]
    dim = HEAD_DIM
    n_heads = q_ref.shape[1] // dim
    part = tok // n_head
    n_near = len(groups) - 1
    scale = 1.0 / dim**0.5
    lat, lon, head = (lax.axis_index(a) for a in ("lat", "lon", "head"))
    mine = pl.ds(pl.multiple_of(head * part, part), part)

    def at(off, sign):
        return {
            "lat": lax.rem(lat + (sign * off[0]) % n_lat, n_lat),
            "lon": lax.rem(lon + (sign * off[1]) % n_lon, n_lon),
            "head": head,
        }

    def fellow(step):
        return {"lat": lat, "lon": lon, "head": lax.rem(head + step, n_head)}

    def send(src, dst, s_sem, r_sem, to):
        copy = pltpu.make_async_remote_copy(
            src_ref=src, dst_ref=dst, send_sem=s_sem, recv_sem=r_sem, device_id=to, device_id_type=MESH
        )
        copy.start()
        return copy

    barrier = pltpu.get_barrier_semaphore()
    for off, _ in groups[1:]:
        pl.semaphore_signal(barrier, inc=1, device_id=at(off, -1), device_id_type=MESH)
    for step in range(1, n_head):
        pl.semaphore_signal(barrier, inc=1, device_id=fellow(step), device_id_type=MESH)
    def fold(x):
        return x.reshape(x.shape[0] // 8, 8, x.shape[1])

    above = jnp.zeros((dim, tok), BF16)

    def prepare(i, carry):
        cols = pl.ds(pl.multiple_of(i * 2 * dim, 2 * dim), 2 * dim)
        q_two = (q_ref[:, cols].astype(F32) * scale).astype(BF16).T
        d_two = d_ref[:, cols].T
        for k in range(2):
            h = 2 * i + k
            rhs[h, :dim, :tok] = q_two[k * dim : (k + 1) * dim]
            rhs[h, dim:, :tok] = above
            rhs[h, :dim, tok:] = above
            rhs[h, dim:, tok:] = d_two[k * dim : (k + 1) * dim]
        for k in range(2):
            h = 2 * i + k
            top = None
            for r in range(0, tok, piece):
                s = jnp.dot(kv_ref[pl.ds(r, piece)], rhs[h, :, :tok], preferred_element_type=F32)
                so[h, pl.ds(r, piece), :tok] = s
                m = jnp.max(fold(s), axis=0)
                top = m if top is None else jnp.maximum(top, m)
                so[h, pl.ds(r, piece), tok:] = jnp.dot(
                    kv_ref[pl.ds(r, piece)], rhs[h, :, tok:], preferred_element_type=F32
                )
            mo[h] = top
        return carry

    piece = tok
    half = 3 * n_heads // 8
    keyt[...] = kv_ref[...].T[:dim]
    prepare(0, 0)
    pl.semaphore_wait(barrier, n_near + n_head - 1)
    kv_copies = [
        send(kv_ref.at[mine], kvb.at[b, mine], kv_send.at[b], kv_recv.at[b], at(off, -1))
        for b, (off, _) in enumerate(groups[1:])
    ]
    lax.fori_loop(1, half, prepare, 0)
    fw_copies = []
    for b in range(n_near):
        kv_copies[b].wait()
        for step in range(1, n_head):
            fw_copies.append(
                send(kvb.at[b, mine], kvb.at[b, mine], fw_send.at[b, step], fw_recv.at[b, step], fellow(step))
            )
    lax.fori_loop(half, n_heads // 2, prepare, 0)
    for copy in fw_copies:
        copy.wait()
    for b in range(n_near):
        keyn[:, pl.ds(b * tok, tok)] = (kvb[b].T[:dim].astype(F32) * groups[1 + b][1]).astype(BF16)

    def score_tasks(h, s_ref, m_ref):
        tasks = []
        for b in range(n_near):
            for r in range(0, tok, piece):

                def score(b=b, r=r):
                    s = jnp.dot(kvb[b, pl.ds(r, piece)], rhs[h, :, :tok], preferred_element_type=F32)
                    s_ref[pl.ds(b * tok + r, piece), :tok] = s
                    m = jnp.max(fold(s), axis=0)
                    m_ref[...] = m if b + r == 0 else jnp.maximum(m_ref[...], m)

                def gain(b=b, r=r):
                    s_ref[pl.ds(b * tok + r, piece), tok:] = jnp.dot(
                        kvb[b, pl.ds(r, piece)], rhs[h, :, tok:], preferred_element_type=F32
                    )

                tasks += [score, gain]
        return tasks

    rows, width = 64, tok // 2

    def near_rows(b, r):
        return pl.ds((b - 1) * tok + r, rows)

    chunks = [(b, r) for b in range(n_near + 1) for r in range(0, tok, rows)]

    def first_tasks(h, s_ref, m_ref, p_ref, f_ref):
        tasks = []
        for t in range(0, tok, width):
            s_cols, d_cols = pl.ds(t, width), pl.ds(tok + t, width)
            state = {}

            def begin(state=state, s_cols=s_cols):
                state["top"] = jnp.max(jnp.maximum(mo[h, :, s_cols], m_ref[:, s_cols]), axis=0, keepdims=True)
                state["sums"], state["dots"] = 0.0, 0.0

            def first(b, r, state=state, s_cols=s_cols, d_cols=d_cols):
                if b == 0:
                    s, dp = so[h, pl.ds(r, rows), s_cols], so[h, pl.ds(r, rows), d_cols]
                else:
                    s, dp = s_ref[near_rows(b, r), s_cols], s_ref[near_rows(b, r), d_cols]
                e = jnp.exp(s - state["top"])
                if b == 0:
                    pown[h, pl.ds(r, rows), d_cols] = e.astype(BF16)
                else:
                    p_ref[near_rows(b, r), d_cols] = e.astype(BF16)
                if r == 0:
                    state["l"], state["e"] = 0.0, 0.0
                state["l"] += jnp.sum(fold(e), axis=0)
                state["e"] += jnp.sum(fold(e * dp), axis=0)
                if r + rows == tok:
                    state["sums"] += groups[b][1] * state["l"]
                    state["dots"] += groups[b][1] * state["e"]

            def finish(state=state, s_cols=s_cols):
                total = jnp.sum(state["sums"], axis=0, keepdims=True)
                delta[:, s_cols] = jnp.sum(state["dots"], axis=0, keepdims=True) / total
                invs[h, :, s_cols] = 1.0 / total

            tasks.append(begin)
            tasks += [functools.partial(first, b, r) for b, r in chunks]
            tasks.append(finish)
        return tasks

    def second_tasks(h, s_ref, m_ref, p_ref, f_ref):
        tasks = []
        for t in range(0, tok, width):
            s_cols, d_cols = pl.ds(t, width), pl.ds(tok + t, width)

            def features(t=t, s_cols=s_cols, d_cols=d_cols):
                inv = invs[h, :, s_cols]
                for base, cols in ((t, s_cols), (tok + t, d_cols)):
                    scaled = (rhs[h, :, cols].astype(F32) * inv).astype(BF16).T
                    f_ref[pl.ds(base, width)] = scaled
                    feats[h, pl.ds(base, width)] = scaled

            def second(b, r, s_cols=s_cols, d_cols=d_cols):
                if b == 0:
                    low, dp = pown[h, pl.ds(r, rows), d_cols], so[h, pl.ds(r, rows), d_cols]
                else:
                    low, dp = p_ref[near_rows(b, r), d_cols], s_ref[near_rows(b, r), d_cols]
                ds = (low.astype(F32) * (dp - delta[:, s_cols])).astype(BF16)
                if b == 0:
                    pown[h, pl.ds(r, rows), s_cols] = ds
                else:
                    p_ref[near_rows(b, r), s_cols] = ds

            tasks.append(features)
            tasks += [functools.partial(second, b, r) for b, r in chunks]
        return tasks

    def grad_tasks(h, p_ref, f_ref):
        tasks = []
        for b in range(n_near):
            for r in range(0, tok, piece):

                def grad(b=b, r=r):
                    acc[b, pl.ds(r, piece)] += jnp.dot(
                        p_ref[pl.ds(b * tok + r, piece)], f_ref[...], preferred_element_type=F32
                    )

                tasks.append(grad)

        def to_queries():
            dqn[h] = jnp.dot(keyn[...], p_ref[:, :tok], preferred_element_type=F32)

        if n_near:
            tasks.append(to_queries)
        return tasks

    acc[...] = jnp.zeros_like(acc)
    if not n_near:
        dqn[...] = jnp.zeros_like(dqn)
        ma[...] = jnp.full_like(ma, -jnp.inf)
        mb[...] = jnp.full_like(mb, -jnp.inf)
    even, odd = (sa, ma, pa, fa), (sb, mb, pb, fb)

    def block(*lists):
        @pl.when(lat >= 0)
        def _():
            interleave(*lists)

    if n_near > DEEP:

        def one(h, carry):
            block(score_tasks(h, sa, ma))
            block(first_tasks(h, *even))
            block(second_tasks(h, *even))
            block(grad_tasks(h, pa, fa))
            return carry

        lax.fori_loop(0, n_heads, one, 0)
    else:
        block(score_tasks(0, sa, ma))
        block(first_tasks(0, *even), score_tasks(1, sb, mb))
        block(second_tasks(0, *even))

        def pair(i, carry):
            h = 2 * i + 1
            block(first_tasks(h, *odd), score_tasks(h + 1, sa, ma))
            block(second_tasks(h, *odd), grad_tasks(h - 1, pa, fa))
            block(first_tasks(h + 1, *even), score_tasks(h + 2, sb, mb))
            block(second_tasks(h + 1, *even), grad_tasks(h, pb, fb))
            return carry

        lax.fori_loop(0, n_heads // 2 - 1, pair, 0)
        last = n_heads - 1
        block(first_tasks(last, *odd))
        block(second_tasks(last, *odd), grad_tasks(last - 1, pa, fa))
        block(grad_tasks(last, pb, fb))

    def rows_of(step):
        return pl.ds(pl.multiple_of(lax.rem(head + step, n_head) * part, part), part)

    x_copies = []
    for b in range(n_near):
        for step in range(1, n_head):
            xs[b, step] = (acc[b, rows_of(step)] * groups[1 + b][1]).astype(BF16)
            x_copies.append(send(xs.at[b, step], xr.at[b, step], xs_send.at[b, step], xs_recv.at[b, step], fellow(step)))

    def own_pair(i, carry):
        for r in range(0, tok, piece):
            kept[pl.ds(r, piece)] += jnp.dot(
                pown[2 * i, pl.ds(r, piece)], feats[2 * i], preferred_element_type=F32
            ) + jnp.dot(pown[2 * i + 1, pl.ds(r, piece)], feats[2 * i + 1], preferred_element_type=F32)
        return carry

    def own_queries(i, carry):
        both = []
        for h in (2 * i, 2 * i + 1):
            dq = jnp.dot(keyt[...], pown[h, :, :tok], preferred_element_type=F32) * groups[0][1] + dqn[h]
            both.append((dq * invs[h]).astype(BF16))
        cols = pl.ds(pl.multiple_of(i * 2 * dim, 2 * dim), 2 * dim)
        dq_ref[:, cols] = jnp.concatenate(both, axis=0).T
        return carry

    kept[...] = jnp.zeros_like(kept)
    lax.fori_loop(0, n_heads // 8, own_pair, 0)
    g_copies = []
    for copy in x_copies:
        copy.wait()
    for b, (off, times) in enumerate(groups[1:]):
        total = acc[b, mine] * times
        for step in range(1, n_head):
            total += xr[b, step].astype(F32)
        gs[b] = total.astype(BF16)
        g_copies.append(send(gs.at[b], gr.at[b], g_send.at[b], g_recv.at[b], at(off, 1)))
    lax.fori_loop(n_heads // 8, n_heads // 2, own_pair, 0)
    o_copies = []
    for step in range(1, n_head):
        xos[step] = kept[rows_of(step)]
        o_copies.append(send(xos.at[step], xor_.at[step], o_send.at[step], o_recv.at[step], fellow(step)))
    lax.fori_loop(0, n_heads // 2, own_queries, 0)
    for copy in o_copies:
        copy.wait()
    total = kept[mine]
    for step in range(1, n_head):
        total += xor_[step]
    dkv_ref[0] = total * groups[0][1]
    total = jnp.zeros_like(total)
    for b, copy in enumerate(g_copies):
        copy.wait()
        total += gr[b].astype(F32)
    dkv_ref[1] = total


def local(sizes, queries, key_value, dout):
    n_head = sizes[2]
    tok, width = key_value.shape[2:]
    n_heads = queries.shape[3] // HEAD_DIM
    groups = tile_groups(sizes[0], sizes[1])
    near = max(len(groups) - 1, 1)
    second = near * tok if near <= DEEP else 16
    part = tok // n_head
    vmem = pl.BlockSpec(memory_space=pltpu.VMEM)
    dma = pltpu.SemaphoreType.DMA
    keys = len(groups) * tok
    dq, dkv = pl.pallas_call(
        functools.partial(kernel, groups, sizes),
        out_shape=(
            jax.ShapeDtypeStruct((tok, n_heads * HEAD_DIM), BF16),
            jax.ShapeDtypeStruct((2, part, width), F32),
        ),
        in_specs=[vmem] * 3,
        out_specs=(vmem, vmem),
        scratch_shapes=[
            pltpu.VMEM((near, tok, width), BF16),
            pltpu.VMEM((n_heads, width, 2 * tok), BF16),
            pltpu.VMEM((n_heads, 2 * tok, width), BF16),
            pltpu.VMEM((n_heads, tok, 2 * tok), F32),
            pltpu.VMEM((near * tok, 2 * tok), F32),
            pltpu.VMEM((second, 2 * tok), F32),
            pltpu.VMEM((n_heads, tok, 2 * tok), BF16),
            pltpu.VMEM((near * tok, 2 * tok), BF16),
            pltpu.VMEM((second, 2 * tok), BF16),
            pltpu.VMEM((2 * tok, width), BF16),
            pltpu.VMEM((2 * tok, width), BF16),
            pltpu.VMEM((n_heads, 8, tok), F32),
            pltpu.VMEM((8, tok), F32),
            pltpu.VMEM((8, tok), F32),
            pltpu.VMEM((near, tok, width), F32),
            pltpu.VMEM((n_heads, HEAD_DIM, tok), F32),
            pltpu.VMEM((n_heads, 1, tok), F32),
            pltpu.VMEM((1, tok), F32),
            pltpu.VMEM((HEAD_DIM, tok), BF16),
            pltpu.VMEM((HEAD_DIM, near * tok), BF16),
            pltpu.VMEM((tok, width), F32),
            pltpu.VMEM((near, n_head, part, width), BF16),
            pltpu.VMEM((near, n_head, part, width), BF16),
            pltpu.VMEM((near, part, width), BF16),
            pltpu.VMEM((near, part, width), BF16),
            pltpu.VMEM((n_head, part, width), F32),
            pltpu.VMEM((n_head, part, width), F32),
            dma((near,)), dma((near,)),
            dma((near, n_head)), dma((near, n_head)),
            dma((near, n_head)), dma((near, n_head)),
            dma((near,)), dma((near,)),
            dma((n_head,)), dma((n_head,)),
        ],
        compiler_params=pltpu.CompilerParams(
            collective_id=0, has_side_effects=True, vmem_limit_bytes=62 * 2**20
        ),
        cost_estimate=pl.CostEstimate(
            flops=10 * n_heads * tok * keys * HEAD_DIM,
            bytes_accessed=8 * tok * n_heads * HEAD_DIM,
            transcendentals=n_heads * tok * keys,
        ),
    )(queries[0, 0], key_value[0, 0], dout[0, 0])
    return (dq * jnp.asarray(1.0 / HEAD_DIM**0.5, BF16))[None, None], (dkv[0] + dkv[1])[None, None]


def solution(mesh):
    sizes = tuple(mesh.shape[a] for a in ("lat", "lon", "head"))
    placed = P("lat", "lon", None, "head")
    return jax.shard_map(
        functools.partial(local, sizes),
        mesh=mesh,
        in_specs=(placed, P("lat", "lon", None, None), placed),
        out_specs=(placed, P("lat", "lon", "head", None)),
        check_vma=False,
    )
```

```python
import functools

import jax
import jax.numpy as jnp
from jax import lax
from jax.experimental import pallas as pl
from jax.experimental.pallas import tpu as pltpu
from jax.sharding import PartitionSpec as P

HEAD_DIM = 64
REACH = 2
DEEP = 2
MESH = pl.DeviceIdType.MESH
F32 = jnp.float32
BF16 = jnp.bfloat16


def tile_groups(n_lat, n_lon):
    counts = {}
    for dlat, dlon in ((0, 0), (REACH, 0), (-REACH, 0), (0, REACH), (0, -REACH)):
        at = (dlat % n_lat, dlon % n_lon)
        counts[at] = counts.get(at, 0) + 1
    return list(counts.items())


def interleave(*lists):
    ranked = []
    for k, tasks in enumerate(lists):
        ranked += [((j + 0.5) / len(tasks), k, j) for j in range(len(tasks))]
    for _, k, j in sorted(ranked):
        lists[k][j]()


def kernel(
    groups, sizes, q_ref, kv_ref, d_ref, dq_ref, dkv_ref,
    kvb, rhs, feats, so, sa, sb, pown, pa, pb, fa, fb, mo, ma, mb, flat, acc, dqn, invs, delta, keyt, keyn, kept,
    xs, xr, gs, gr, xos, xor_,
    kv_send, kv_recv, fw_send, fw_recv, xs_send, xs_recv, g_send, g_recv, o_send, o_recv,
):
    n_lat, n_lon, n_head = sizes
    tok = kv_ref.shape[0]
    dim = HEAD_DIM
    n_heads = q_ref.shape[1] // dim
    part = tok // n_head
    n_near = len(groups) - 1
    scale = 1.0 / dim**0.5
    lat, lon, head = (lax.axis_index(a) for a in ("lat", "lon", "head"))
    mine = pl.ds(pl.multiple_of(head * part, part), part)

    def at(off, sign):
        return {
            "lat": lax.rem(lat + (sign * off[0]) % n_lat, n_lat),
            "lon": lax.rem(lon + (sign * off[1]) % n_lon, n_lon),
            "head": head,
        }

    def fellow(step):
        return {"lat": lat, "lon": lon, "head": lax.rem(head + step, n_head)}

    def send(src, dst, s_sem, r_sem, to):
        copy = pltpu.make_async_remote_copy(
            src_ref=src, dst_ref=dst, send_sem=s_sem, recv_sem=r_sem, device_id=to, device_id_type=MESH
        )
        copy.start()
        return copy

    barrier = pltpu.get_barrier_semaphore()
    for off, _ in groups[1:]:
        pl.semaphore_signal(barrier, inc=1, device_id=at(off, -1), device_id_type=MESH)
    for step in range(1, n_head):
        pl.semaphore_signal(barrier, inc=1, device_id=fellow(step), device_id_type=MESH)
    def fold(x):
        return x.reshape(x.shape[0] // 8, 8, x.shape[1])

    def across(a, b):
        return lax.dot_general(a, b, (((1,), (1,)), ((), ())), preferred_element_type=F32)

    above = jnp.zeros((dim, tok), BF16)

    def prepare(i, carry):
        cols = pl.ds(pl.multiple_of(i * 2 * dim, 2 * dim), 2 * dim)
        q_two = (q_ref[:, cols].astype(F32) * scale).astype(BF16).T
        d_two = d_ref[:, cols].T
        for k in range(2):
            h = 2 * i + k
            rhs[h, :dim, :tok] = q_two[k * dim : (k + 1) * dim]
            rhs[h, dim:, :tok] = above
            rhs[h, :dim, tok:] = above
            rhs[h, dim:, tok:] = d_two[k * dim : (k + 1) * dim]
        for k in range(2):
            h = 2 * i + k
            top = None
            for r in range(0, tok, piece):
                s = jnp.dot(kv_ref[pl.ds(r, piece)], rhs[h, :, :tok], preferred_element_type=F32)
                so[h, pl.ds(r, piece), :tok] = s
                m = jnp.max(fold(s), axis=0)
                top = m if top is None else jnp.maximum(top, m)
                so[h, pl.ds(r, piece), tok:] = jnp.dot(
                    kv_ref[pl.ds(r, piece)], rhs[h, :, tok:], preferred_element_type=F32
                )
            mo[h] = top
        return carry

    piece = tok
    half = 3 * n_heads // 8
    keyt[...] = kv_ref[...].T[:dim]
    prepare(0, 0)
    pl.semaphore_wait(barrier, n_near + n_head - 1)
    kv_copies = [
        send(kv_ref.at[mine], kvb.at[b, mine], kv_send.at[b], kv_recv.at[b], at(off, -1))
        for b, (off, _) in enumerate(groups[1:])
    ]
    lax.fori_loop(1, half, prepare, 0)
    fw_copies = []
    for b in range(n_near):
        kv_copies[b].wait()
        for step in range(1, n_head):
            fw_copies.append(
                send(kvb.at[b, mine], kvb.at[b, mine], fw_send.at[b, step], fw_recv.at[b, step], fellow(step))
            )
    lax.fori_loop(half, n_heads // 2, prepare, 0)
    for copy in fw_copies:
        copy.wait()
    for b in range(n_near):
        keyn[:, pl.ds(b * tok, tok)] = (kvb[b].T[:dim].astype(F32) * groups[1 + b][1]).astype(BF16)

    def score_tasks(h, s_ref, m_ref):
        tasks = []
        for b in range(n_near):
            for r in range(0, tok, piece):

                def score(b=b, r=r):
                    s = jnp.dot(kvb[b, pl.ds(r, piece)], rhs[h, :, :tok], preferred_element_type=F32)
                    s_ref[pl.ds(b * tok + r, piece), :tok] = s
                    m = jnp.max(fold(s), axis=0)
                    m_ref[...] = m if b + r == 0 else jnp.maximum(m_ref[...], m)

                def gain(b=b, r=r):
                    s_ref[pl.ds(b * tok + r, piece), tok:] = jnp.dot(
                        kvb[b, pl.ds(r, piece)], rhs[h, :, tok:], preferred_element_type=F32
                    )

                tasks += [score, gain]
        return tasks

    rows, width = 64, tok // 2

    def near_rows(b, r):
        return pl.ds((b - 1) * tok + r, rows)

    chunks = [(b, r) for b in range(n_near + 1) for r in range(0, tok, rows)]

    def first_tasks(h, s_ref, m_ref, p_ref, f_ref):
        tasks = []
        for t in range(0, tok, width):
            s_cols, d_cols = pl.ds(t, width), pl.ds(tok + t, width)
            state = {}

            def begin(state=state, s_cols=s_cols):
                state["top"] = jnp.max(jnp.maximum(mo[h, :, s_cols], m_ref[:, s_cols]), axis=0, keepdims=True)
                state["sums"], state["dots"] = 0.0, 0.0

            def first(b, r, state=state, s_cols=s_cols, d_cols=d_cols):
                if b == 0:
                    s, dp = so[h, pl.ds(r, rows), s_cols], so[h, pl.ds(r, rows), d_cols]
                else:
                    s, dp = s_ref[near_rows(b, r), s_cols], s_ref[near_rows(b, r), d_cols]
                e = jnp.exp(s - state["top"])
                if b == 0:
                    pown[h, pl.ds(r, rows), d_cols] = e.astype(BF16)
                else:
                    p_ref[near_rows(b, r), d_cols] = e.astype(BF16)
                if r == 0:
                    state["l"], state["e"] = 0.0, 0.0
                state["l"] += jnp.sum(fold(e), axis=0)
                state["e"] += jnp.sum(fold(e * dp), axis=0)
                if r + rows == tok:
                    state["sums"] += groups[b][1] * state["l"]
                    state["dots"] += groups[b][1] * state["e"]

            def finish(state=state, s_cols=s_cols):
                total = jnp.sum(state["sums"], axis=0, keepdims=True)
                delta[:, s_cols] = jnp.sum(state["dots"], axis=0, keepdims=True) / total
                invs[h, :, s_cols] = 1.0 / total

            tasks.append(begin)
            tasks += [functools.partial(first, b, r) for b, r in chunks]
            tasks.append(finish)
        return tasks

    def second_tasks(h, s_ref, m_ref, p_ref, f_ref):
        tasks = []
        for t in range(0, tok, width):
            s_cols, d_cols = pl.ds(t, width), pl.ds(tok + t, width)

            def features(t=t, s_cols=s_cols, d_cols=d_cols):
                inv = invs[h, :, s_cols]
                for base, cols in ((t, s_cols), (tok + t, d_cols)):
                    scaled = (rhs[h, :, cols].astype(F32) * inv).astype(BF16)
                    f_ref[:, pl.ds(base, width)] = scaled
                    feats[h, :, pl.ds(base, width)] = scaled

            def second(b, r, s_cols=s_cols, d_cols=d_cols):
                if b == 0:
                    low, dp = pown[h, pl.ds(r, rows), d_cols], so[h, pl.ds(r, rows), d_cols]
                else:
                    low, dp = p_ref[near_rows(b, r), d_cols], s_ref[near_rows(b, r), d_cols]
                ds = (low.astype(F32) * (dp - delta[:, s_cols])).astype(BF16)
                if b == 0:
                    pown[h, pl.ds(r, rows), s_cols] = ds
                else:
                    p_ref[near_rows(b, r), s_cols] = ds

            tasks.append(features)
            tasks += [functools.partial(second, b, r) for b, r in chunks]
        return tasks

    def grad_tasks(h, p_ref, f_ref):
        tasks = []
        for b in range(n_near):
            for r in range(0, tok, piece):

                def grad(b=b, r=r):
                    flat[b, :, pl.ds(r, piece)] += across(f_ref[...], p_ref[pl.ds(b * tok + r, piece)])

                tasks.append(grad)

        def to_queries():
            dqn[h] = jnp.dot(keyn[...], p_ref[:, :tok], preferred_element_type=F32)

        if n_near:
            tasks.append(to_queries)
        return tasks

    flat[...] = jnp.zeros_like(flat)
    if not n_near:
        dqn[...] = jnp.zeros_like(dqn)
        ma[...] = jnp.full_like(ma, -jnp.inf)
        mb[...] = jnp.full_like(mb, -jnp.inf)
    even, odd = (sa, ma, pa, fa), (sb, mb, pb, fb)

    def block(*lists):
        @pl.when(lat >= 0)
        def _():
            interleave(*lists)

    if n_near > DEEP:

        def one(h, carry):
            block(score_tasks(h, sa, ma))
            block(first_tasks(h, *even))
            block(second_tasks(h, *even))
            block(grad_tasks(h, pa, fa))
            return carry

        lax.fori_loop(0, n_heads, one, 0)
    else:
        block(score_tasks(0, sa, ma))
        block(first_tasks(0, *even), score_tasks(1, sb, mb))
        block(second_tasks(0, *even))

        def pair(i, carry):
            h = 2 * i + 1
            block(first_tasks(h, *odd), score_tasks(h + 1, sa, ma))
            block(second_tasks(h, *odd), grad_tasks(h - 1, pa, fa))
            block(first_tasks(h + 1, *even), score_tasks(h + 2, sb, mb))
            block(second_tasks(h + 1, *even), grad_tasks(h, pb, fb))
            return carry

        lax.fori_loop(0, n_heads // 2 - 1, pair, 0)
        last = n_heads - 1
        block(first_tasks(last, *odd))
        block(second_tasks(last, *odd), grad_tasks(last - 1, pa, fa))
        block(grad_tasks(last, pb, fb))

    for b in range(n_near):
        acc[b] = flat[b].T

    def rows_of(step):
        return pl.ds(pl.multiple_of(lax.rem(head + step, n_head) * part, part), part)

    x_copies = []
    for b in range(n_near):
        for step in range(1, n_head):
            xs[b, step] = (acc[b, rows_of(step)] * groups[1 + b][1]).astype(BF16)
            x_copies.append(send(xs.at[b, step], xr.at[b, step], xs_send.at[b, step], xs_recv.at[b, step], fellow(step)))

    def own_pair(i, carry):
        for h in (2 * i, 2 * i + 1):
            flat[0] += across(feats[h], pown[h])
        return carry

    def own_queries(i, carry):
        both = []
        for h in (2 * i, 2 * i + 1):
            dq = jnp.dot(keyt[...], pown[h, :, :tok], preferred_element_type=F32) * groups[0][1] + dqn[h]
            both.append((dq * invs[h]).astype(BF16))
        cols = pl.ds(pl.multiple_of(i * 2 * dim, 2 * dim), 2 * dim)
        dq_ref[:, cols] = jnp.concatenate(both, axis=0).T
        return carry

    flat[0] = jnp.zeros_like(flat[0])
    lax.fori_loop(0, n_heads // 8, own_pair, 0)
    g_copies = []
    for copy in x_copies:
        copy.wait()
    for b, (off, times) in enumerate(groups[1:]):
        total = acc[b, mine] * times
        for step in range(1, n_head):
            total += xr[b, step].astype(F32)
        gs[b] = total.astype(BF16)
        g_copies.append(send(gs.at[b], gr.at[b], g_send.at[b], g_recv.at[b], at(off, 1)))
    lax.fori_loop(n_heads // 8, n_heads // 2, own_pair, 0)
    kept[...] = flat[0].T
    o_copies = []
    for step in range(1, n_head):
        xos[step] = kept[rows_of(step)]
        o_copies.append(send(xos.at[step], xor_.at[step], o_send.at[step], o_recv.at[step], fellow(step)))
    lax.fori_loop(0, n_heads // 2, own_queries, 0)
    for copy in o_copies:
        copy.wait()
    total = kept[mine]
    for step in range(1, n_head):
        total += xor_[step]
    dkv_ref[0] = total * groups[0][1]
    total = jnp.zeros_like(total)
    for b, copy in enumerate(g_copies):
        copy.wait()
        total += gr[b].astype(F32)
    dkv_ref[1] = total


def local(sizes, queries, key_value, dout):
    n_head = sizes[2]
    tok, width = key_value.shape[2:]
    n_heads = queries.shape[3] // HEAD_DIM
    groups = tile_groups(sizes[0], sizes[1])
    near = max(len(groups) - 1, 1)
    second = near * tok if near <= DEEP else 16
    part = tok // n_head
    vmem = pl.BlockSpec(memory_space=pltpu.VMEM)
    dma = pltpu.SemaphoreType.DMA
    keys = len(groups) * tok
    dq, dkv = pl.pallas_call(
        functools.partial(kernel, groups, sizes),
        out_shape=(
            jax.ShapeDtypeStruct((tok, n_heads * HEAD_DIM), BF16),
            jax.ShapeDtypeStruct((2, part, width), F32),
        ),
        in_specs=[vmem] * 3,
        out_specs=(vmem, vmem),
        scratch_shapes=[
            pltpu.VMEM((near, tok, width), BF16),
            pltpu.VMEM((n_heads, width, 2 * tok), BF16),
            pltpu.VMEM((n_heads, width, 2 * tok), BF16),
            pltpu.VMEM((n_heads, tok, 2 * tok), F32),
            pltpu.VMEM((near * tok, 2 * tok), F32),
            pltpu.VMEM((second, 2 * tok), F32),
            pltpu.VMEM((n_heads, tok, 2 * tok), BF16),
            pltpu.VMEM((near * tok, 2 * tok), BF16),
            pltpu.VMEM((second, 2 * tok), BF16),
            pltpu.VMEM((width, 2 * tok), BF16),
            pltpu.VMEM((width, 2 * tok), BF16),
            pltpu.VMEM((n_heads, 8, tok), F32),
            pltpu.VMEM((8, tok), F32),
            pltpu.VMEM((8, tok), F32),
            pltpu.VMEM((near, width, tok), F32),
            pltpu.VMEM((near, tok, width), F32),
            pltpu.VMEM((n_heads, HEAD_DIM, tok), F32),
            pltpu.VMEM((n_heads, 1, tok), F32),
            pltpu.VMEM((1, tok), F32),
            pltpu.VMEM((HEAD_DIM, tok), BF16),
            pltpu.VMEM((HEAD_DIM, near * tok), BF16),
            pltpu.VMEM((tok, width), F32),
            pltpu.VMEM((near, n_head, part, width), BF16),
            pltpu.VMEM((near, n_head, part, width), BF16),
            pltpu.VMEM((near, part, width), BF16),
            pltpu.VMEM((near, part, width), BF16),
            pltpu.VMEM((n_head, part, width), F32),
            pltpu.VMEM((n_head, part, width), F32),
            dma((near,)), dma((near,)),
            dma((near, n_head)), dma((near, n_head)),
            dma((near, n_head)), dma((near, n_head)),
            dma((near,)), dma((near,)),
            dma((n_head,)), dma((n_head,)),
        ],
        compiler_params=pltpu.CompilerParams(
            collective_id=0, has_side_effects=True, vmem_limit_bytes=62 * 2**20
        ),
        cost_estimate=pl.CostEstimate(
            flops=10 * n_heads * tok * keys * HEAD_DIM,
            bytes_accessed=8 * tok * n_heads * HEAD_DIM,
            transcendentals=n_heads * tok * keys,
        ),
    )(queries[0, 0], key_value[0, 0], dout[0, 0])
    return (dq * jnp.asarray(1.0 / HEAD_DIM**0.5, BF16))[None, None], (dkv[0] + dkv[1])[None, None]


def solution(mesh):
    sizes = tuple(mesh.shape[a] for a in ("lat", "lon", "head"))
    placed = P("lat", "lon", None, "head")
    return jax.shard_map(
        functools.partial(local, sizes),
        mesh=mesh,
        in_specs=(placed, P("lat", "lon", None, None), placed),
        out_specs=(placed, P("lat", "lon", "head", None)),
        check_vma=False,
    )
```
